32 devices in a mesh: groups: 1, epouter: 16 (over z, y, core), epinner: 2 (over x).
Axes of the slice: x: 2, y: 2, z: 4, core: 2. Of those that a mesh axis runs over, the one named last changes fastest.
Arguments:
- tokens: bfloat16 [1024, 7168], P(('groups', 'epouter'), 'epinner'), may hold values from -6 to 6
- expert_ids: int32 [1024, 2], P(('groups', 'epouter')), may hold values from 0 to 3, all different within a row; in each aligned block of 64 rows (0 to 63, 64 to 127, ...) at most 48 rows name the same one
- route_weight: float32 [1024, 2], P(('groups', 'epouter')), may hold values from 0.1 to 0.5
- w_gate: bfloat16 [16, 7168, 384], P('epouter', 'epinner'), may hold values from -0.0625 to 0.0625
- w_up: bfloat16 [16, 7168, 384], P('epouter', 'epinner'), may hold values from -0.0625 to 0.0625
- w_down: bfloat16 [16, 384, 7168], P('epouter', None, 'epinner'), may hold values from -0.15625 to 0.15625
Outputs:
- moe_out: bfloat16 [1024, 7168], P(('groups', 'epouter'), 'epinner')
The draws below stay inside these ranges and needn't reach their ends.
Inputs may be any that keep to these rules, and one draw needn't show every extreme that they name: `expert_ids`: each row names 2 different experts; in each aligned block of 64 rows (the rows of one index of epouter) no expert is named by more than 48 rows, and in some block one expert is named by exactly 48 rows.
All inputs are finite; a program needn't handle non-finite values.
Results may differ from the reference program's by a relative error of at most 0.0058.
Values may be sent and summed in bfloat16 or wider, within the bound.
A program may use at most 64 MiB of HBM per device.

```python
import math
import jax
import jax.numpy as jnp
import numpy as np
from jax import lax

D = 7168
MOE_HID = 1536
SLICES = 4
HID_DEV = 384
BLOCK = 64
EXPERTS = 4
TOP = 2
CAP = 48
TOKENS = 1024
N_EPOUTER = 16


def levels(key, shape, shards, low, largest):
    def one(axis_at, parts):
        draws = jax.random.uniform(jax.random.fold_in(jax.random.fold_in(key, 6), axis_at), (parts,), jnp.float32, low / len(shards), largest / len(shards))
        return jnp.repeat(jnp.exp(draws), shape[axis_at] // parts).reshape((-1,) + (1,) * (len(shape) - axis_at - 1))

    gain = one(*shards[0])
    for cut in shards[1:]:
        gain = gain * one(*cut)
    return gain


def routed_block(rng, own, number, rows, number_of, top, most, slope):
    ranking = jax.random.permutation(rng, number_of)
    packed, ordinary = portions_of(number_of, rows * top, most, slope, True), portions_of(number_of, rows * top, most, slope, False)
    places = jnp.arange(number_of)

    def named(tallies, offset_by):
        used = int((tallies > 0).sum())
        fixed = max(1, used // 4)
        passed = fixed + (places - fixed + offset_by * (used - fixed)) % max(1, number_of - fixed)
        return jnp.zeros((number_of,), jnp.int32).at[ranking[jnp.where(places < fixed, places, passed)]].set(jnp.asarray(tallies, jnp.int32))

    tallies = jnp.where(number % 4 == 0, named(packed, number // 4), named(ordinary, number - number // 4 - 1))
    mixed = jax.random.permutation(jax.random.fold_in(own, 3), number_of)
    source_of, taker = mixed[0:number_of // 2 * 2:2], mixed[1:number_of // 2 * 2:2]
    slack = jnp.minimum(tallies[source_of] - 1, most - tallies[taker]) // 2
    slack = jnp.where((source_of == ranking[0]) | (taker == ranking[0]) | (tallies[taker] == 0), 0, jnp.maximum(slack, 0))
    passed = jax.random.randint(jax.random.fold_in(own, 4), (number_of // 2,), 0, 1 << 20) % (slack + 1)
    tallies = tallies.at[source_of].add(-passed).at[taker].add(passed)
    members = jnp.searchsorted(jnp.cumsum(tallies), jnp.arange(rows * top), side="right").astype(jnp.int32)
    table = members.reshape(top, rows).T
    table = table[jax.random.permutation(jax.random.fold_in(own, 1), rows)]
    offset_by = jax.random.randint(jax.random.fold_in(own, 2), (rows, 1), 0, top)
    return jnp.take_along_axis(table, (jnp.arange(top)[None, :] + offset_by) % top, axis=1)


def portions_of(number_of, total, reach, lean, full):
    loads = [(1 << 20) // math.isqrt(standing ** lean) + 1 for standing in range(1, number_of + 1)]
    largest = reach if full else min(reach, max(-(-total // number_of), total * loads[0] // sum(loads)))
    least = 1 if total - largest >= number_of - 1 else 0
    holding, spare = [largest] + [least] * (number_of - 1), total - largest - least * (number_of - 1)
    while spare > 0:
        movable = [i for i in range(1, number_of) if holding[i] < largest] or [i for i in range(1, number_of) if holding[i] < reach]
        mass, left = sum([loads[i] for i in movable]), spare
        for i in movable:
            extra = min(reach - holding[i], max(1, left * loads[i] // mass), spare)
            holding[i] = holding[i] + extra
            spare = spare - extra
    return np.array(holding)


def centred(own_key, dims, width, bound, cuts=(), kind=jnp.bfloat16):
    factor_of = levels(own_key, dims, cuts, -0.22, 0.18) if cuts else 1.0
    array = jax.random.normal(own_key, dims, jnp.float32) * width * factor_of
    return jnp.minimum(jnp.maximum(array, -bound), bound).astype(kind)


def setup_inputs(seed: int = 0, part: int = 0) -> dict:
    seeds = jax.random.split(jax.random.key(seed), 7)
    part_keys = jax.random.split(jax.random.fold_in(seeds[6], part), 7)
    tokens = centred(part_keys[0], (TOKENS, D), 1.0, 6.0, ((0, 16), (1, 2)))
    expert_ids_keys = jax.random.split(jax.random.fold_in(part_keys[1], 1), TOKENS // BLOCK)
    expert_ids_turns = jax.random.permutation(jax.random.fold_in(part_keys[1], 3), TOKENS // BLOCK)
    expert_ids = jax.vmap(lambda own, number: routed_block(jax.random.fold_in(part_keys[1], 2), own, number, BLOCK, EXPERTS, TOP, CAP, 2))(expert_ids_keys, expert_ids_turns).reshape((TOKENS, TOP))
    route_weight = jnp.clip(0.1 + 0.4 * jax.random.uniform(part_keys[2], (TOKENS, TOP), jnp.float32) ** levels(part_keys[2], (TOKENS, TOP), ((0, 16),), -0.2, 0.2), 0.1, 0.5)
    w_gate = centred(seeds[3], (EXPERTS * SLICES, D, HID_DEV), D ** -0.5, 0.0625, ((0, 16), (1, 2)))
    w_up = centred(seeds[4], (EXPERTS * SLICES, D, HID_DEV), D ** -0.5, 0.0625, ((0, 16), (1, 2)))
    w_down = centred(seeds[5], (EXPERTS * SLICES, HID_DEV, D), MOE_HID ** -0.5, 0.15625, ((0, 16), (2, 2)))
    return {"tokens": tokens, "expert_ids": expert_ids, "route_weight": route_weight, "w_gate": w_gate, "w_up": w_up, "w_down": w_down}


def reference(tokens, expert_ids, route_weight, w_gate, w_up, w_down):
    experts = w_gate.shape[0] // SLICES
    limit = min(tokens.shape[0], N_EPOUTER * CAP)

    def add_expert(total, expert):
        coefficient = jnp.sum(jnp.where(expert_ids == expert, route_weight, 0.0), axis=1)
        chosen = jnp.sum((expert_ids == expert).astype(jnp.int32), axis=1)
        order = jnp.argsort(-chosen, stable=True)[:limit].astype(jnp.int32)
        rows = jnp.take(tokens, order, axis=0)
        expert_sum = jnp.zeros((limit, tokens.shape[1]), jnp.float32)
        for slice_index in range(SLICES):
            weight_index = (expert * SLICES + slice_index).astype(jnp.int32)
            gate_matrix = lax.dynamic_index_in_dim(w_gate, weight_index, 0, keepdims=False)
            up_matrix = lax.dynamic_index_in_dim(w_up, weight_index, 0, keepdims=False)
            down_matrix = lax.dynamic_index_in_dim(w_down, weight_index, 0, keepdims=False)
            gate_part = jnp.dot(rows, gate_matrix, preferred_element_type=jnp.float32)
            up_part = jnp.dot(rows, up_matrix, preferred_element_type=jnp.float32)
            hidden = (jax.nn.silu(gate_part) * up_part).astype(jnp.bfloat16)
            part_out = jnp.dot(hidden, down_matrix, preferred_element_type=jnp.float32).astype(jnp.bfloat16)
            expert_sum = expert_sum + part_out.astype(jnp.float32)
        scaled = jnp.take(coefficient, order, axis=0)[:, None] * expert_sum
        return total.at[order].add(scaled), None

    start = jnp.zeros(tokens.shape, jnp.float32)
    total, unused = lax.scan(add_expert, start, jnp.arange(experts, dtype=jnp.int32))
    return total.astype(jnp.bfloat16)
```

```python
import functools

import jax
import jax.numpy as jnp
from jax import lax
from jax.experimental import pallas as pl
from jax.experimental.pallas import tpu as pltpu
from jax.sharding import PartitionSpec as P

SLICES = 4
MESH = pl.DeviceIdType.MESH
F32 = jnp.float32
BF16 = jnp.bfloat16


def tile_of(width):
    return next(t for t in (512, 256, 128) if width % t == 0)


def each_tile(width, tile, body):
    @pl.loop(0, width // tile)
    def _(i):
        body(pl.ds(pl.multiple_of(i * tile, tile), tile))


def layer_kernel(
    experts, inner, slot,
    tokens, ids, ids_t, weight, w_gate, w_up, w_down, out,
    w_in, w_out, outgoing, rows, own, x_send, x_recv, hidden, part, core_recv,
    y_send, y_recv, z_send, returned,
    w_sem, zs, zr, ys, yr, cs, cr, xs, xr, ps, pr, qs, qr, bs, br,
):
    block, width = tokens.shape
    picks = ids.shape[1]
    hid = w_down.shape[1]
    here = lax.axis_index("epouter")
    expert = here // SLICES
    part_at = here % SLICES
    side = part_at % 2
    sib = part_at + 1 - 2 * side
    flip = lax.rem(part_at + 2, SLICES)
    sib_flip = lax.rem(sib + 2, SLICES)
    base = expert * SLICES
    x_at = lax.axis_index("epinner")
    tile = tile_of(width)

    def at_layer(step):
        return {"epouter": lax.rem(expert + step + experts, experts) * SLICES + part_at}

    to_sib = {"epouter": base + sib}
    to_flip = {"epouter": base + flip}

    def at_inner(step):
        return {"epinner": lax.rem(x_at + step, inner)}

    loads = [
        pltpu.make_async_copy(w_gate.at[0], w_in.at[:, pl.ds(0, hid)], w_sem.at[0]),
        pltpu.make_async_copy(w_up.at[0], w_in.at[:, pl.ds(hid, hid)], w_sem.at[1]),
        pltpu.make_async_copy(w_down.at[0], w_out, w_sem.at[2]),
    ]

    barrier = pltpu.get_barrier_semaphore()
    partners = [at_layer(k) for k in range(1, experts)] + [to_sib, to_flip]
    partners += [at_inner(d) for d in range(1, inner)]
    for partner in partners:
        pl.semaphore_signal(barrier, inc=1, device_id=partner, device_id_type=MESH)

    named_row = lax.rem(expert + lax.broadcasted_iota(jnp.int32, (experts, block), 0), experts)
    chosen_row = jnp.zeros((experts, block), F32)
    for p in range(picks):
        chosen_row += (ids_t[p : p + 1, :] == named_row).astype(F32)
    before = (
        lax.broadcasted_iota(jnp.int32, (block, block), 0)
        < lax.broadcasted_iota(jnp.int32, (block, block), 1)
    ).astype(F32)
    pos_row = jnp.dot(
        chosen_row.astype(BF16), before.astype(BF16), preferred_element_type=F32
    )
    pos_row = jnp.where(chosen_row > 0, pos_row, -1.0)
    slots = lax.broadcasted_iota(jnp.int32, (slot, block), 0).astype(F32)

    def placed(k):
        return jnp.where(pos_row[k : k + 1, :] == slots, 1.0, 0.0).astype(BF16)

    def gather_into(k, target):
        place = placed(k)

        def body(cols):
            target[:, cols] = jnp.dot(
                place, tokens[:, cols], preferred_element_type=F32
            ).astype(BF16)

        each_tile(width, tile, body)

    def remote(src, dst, send, recv, device):
        return pltpu.make_async_remote_copy(
            src_ref=src, dst_ref=dst, send_sem=send, recv_sem=recv,
            device_id=device, device_id_type=MESH,
        )

    def z_out(k):
        return remote(
            outgoing.at[k - 1], rows.at[k, part_at], zs.at[k], zr.at[k], at_layer(k)
        )

    def y_out(k):
        mine = rows.at[k, part_at]
        return remote(mine, mine, ys.at[k], yr.at[k], to_flip)

    def core_out(k, which):
        ref = rows.at[k, part_at if which == 0 else flip]
        return remote(ref, ref, cs.at[k, which], cr.at[k, which], to_sib)

    def x_out(k, d):
        return remote(
            x_send.at[k], x_recv.at[k, d - 1], xs.at[k, d - 1], xr.at[k, d - 1], at_inner(d)
        )

    def core_back(k, which):
        return remote(
            part.at[k, sib if which == 0 else sib_flip], core_recv.at[k, which],
            ps.at[k, which], pr.at[k, which], to_sib,
        )

    def y_back(k):
        return remote(y_send.at[k], y_recv.at[k], qs.at[k], qr.at[k], to_flip)

    def z_back(k):
        return remote(z_send.at[k - 1], returned.at[k], bs.at[k], br.at[k], at_layer(-k))

    gather_into(0, rows.at[0, part_at])
    pl.semaphore_wait(barrier, len(partners))
    y_out(0).start()
    core_out(0, 0).start()
    for k in range(1, experts):
        gather_into(k, outgoing.at[k - 1])
        z_out(k).start()
    for load in loads:
        load.start()

    def arrive(k):
        z_out(k).wait_recv()
        y_out(k).start()
        core_out(k, 0).start()

    def up(k):
        y_out(k).wait_recv()
        core_out(k, 1).start()
        if k == 0:
            loads[0].wait()
            loads[1].wait()
        core_out(k, 0).wait_recv()
        core_out(k, 1).wait_recv()

        def body(cols):
            x = rows[k].reshape(SLICES * slot, width)
            value = jnp.dot(x, w_in[:, cols], preferred_element_type=F32)
            own[k, :, cols] = value
            x_send[k, :, cols] = value.astype(BF16)

        each_tile(2 * hid, 256 if (2 * hid) % 256 == 0 else 128, body)
        for d in range(1, inner):
            x_out(k, d).start()

    def down(k):
        for d in range(1, inner):
            x_out(k, d).wait_recv()
        if k == 0:
            loads[2].wait()

        def act(cols):
            upper = pl.ds(pl.multiple_of(cols.start + hid, 128), cols.size)
            gate = own[k, :, cols]
            lift = own[k, :, upper]
            for d in range(inner - 1):
                gate += x_recv[k, d, :, cols].astype(F32)
                lift += x_recv[k, d, :, upper].astype(F32)
            hidden[:, cols] = (gate / (1.0 + jnp.exp(-gate)) * lift).astype(BF16)

        each_tile(hid, 128, act)

        def body(cols):
            value = jnp.dot(hidden[...], w_out[:, cols], preferred_element_type=F32)
            part[k, :, :, cols] = value.astype(BF16).reshape(SLICES, slot, tile)

        each_tile(width, tile, body)
        core_back(k, 1).start()
        core_back(k, 0).start()

    def fold_core(k):
        core_back(k, 1).wait_recv()

        def body(cols):
            y_send[k, :, cols] = (
                part[k, flip, :, cols].astype(F32) + core_recv[k, 1, :, cols].astype(F32)
            ).astype(BF16)

        each_tile(width, tile, body)
        y_back(k).start()

    def fold_y(k):
        core_back(k, 0).wait_recv()
        y_back(k).wait_recv()
        target = returned.at[0] if k == 0 else z_send.at[k - 1]

        def body(cols):
            target[:, cols] = (
                part[k, part_at, :, cols].astype(F32)
                + core_recv[k, 0, :, cols].astype(F32)
                + y_recv[k, :, cols].astype(F32)
            ).astype(BF16)

        each_tile(width, tile, body)
        if k:
            z_back(k).start()

    for t in range(experts + 3):
        if t + 1 < experts:
            arrive(t + 1)
        if t < experts:
            up(t)
        if 0 <= t - 2 < experts:
            fold_core(t - 2)
        if 0 <= t - 3 < experts:
            fold_y(t - 3)
        if 0 <= t - 1 < experts:
            down(t - 1)

    lanes = experts * slot
    named_col = lax.rem(expert + lax.broadcasted_iota(jnp.int32, (block, experts), 1), experts)
    chosen = jnp.zeros((block, experts), F32)
    coef = jnp.zeros((block, experts), F32)
    for p in range(picks):
        same = ids[:, p : p + 1] == named_col
        chosen += same.astype(F32)
        coef += jnp.where(same, weight[:, p : p + 1], 0.0)
    after = (
        lax.broadcasted_iota(jnp.int32, (block, block), 1)
        < lax.broadcasted_iota(jnp.int32, (block, block), 0)
    ).astype(F32)
    pos = jnp.dot(after.astype(BF16), chosen.astype(BF16), preferred_element_type=F32)
    lane = lax.broadcasted_iota(jnp.int32, (block, lanes), 1)
    spread = jnp.zeros((block, lanes), F32)
    for k in range(experts):
        lane_at = (lane - k * slot).astype(F32)
        hit = (pos[:, k : k + 1] == lane_at) & (lane >= k * slot) & (lane < (k + 1) * slot)
        spread += jnp.where(hit, coef[:, k : k + 1], 0.0)
    high = spread.astype(BF16)
    low = (spread - high.astype(F32)).astype(BF16)
    for k in range(1, experts):
        z_back(k).wait_recv()

    def finish(cols):
        back = returned[:, :, cols].reshape(lanes, tile)
        out[:, cols] = (
            jnp.dot(high, back, preferred_element_type=F32)
            + jnp.dot(low, back, preferred_element_type=F32)
        ).astype(BF16)

    each_tile(width, tile, finish)

    for k in range(experts):
        if k:
            z_out(k).wait_send()
            z_back(k).wait_send()
        y_out(k).wait_send()
        y_back(k).wait_send()
        for which in range(2):
            core_out(k, which).wait_send()
            core_back(k, which).wait_send()
        for d in range(1, inner):
            x_out(k, d).wait_send()


def shards(tokens, expert_ids, route_weight, w_gate, w_up, w_down):
    experts = lax.axis_size("epouter") // SLICES
    inner = lax.axis_size("epinner")
    block, width = tokens.shape
    picks = expert_ids.shape[1]
    hid = w_down.shape[1]
    depth = min(block, 3 * block * picks // (2 * experts))
    slot = -(-depth // 16) * 16
    rows = SLICES * slot
    vmem = pl.BlockSpec(memory_space=pltpu.VMEM)
    hbm = pl.BlockSpec(memory_space=pl.ANY)
    dma = pltpu.SemaphoreType.DMA
    others = max(inner - 1, 1)
    total = experts * rows
    return pl.pallas_call(
        functools.partial(layer_kernel, experts, inner, slot),
        out_shape=jax.ShapeDtypeStruct((block, width), BF16),
        in_specs=[vmem] * 4 + [hbm] * 3,
        out_specs=vmem,
        scratch_shapes=[
            pltpu.VMEM((width, 2 * hid), BF16),
            pltpu.VMEM((hid, width), BF16),
            pltpu.VMEM((max(experts - 1, 1), slot, width), BF16),
            pltpu.VMEM((experts, SLICES, slot, width), BF16),
            pltpu.VMEM((experts, rows, 2 * hid), F32),
            pltpu.VMEM((experts, rows, 2 * hid), BF16),
            pltpu.VMEM((experts, others, rows, 2 * hid), BF16),
            pltpu.VMEM((rows, hid), BF16),
            pltpu.VMEM((experts, SLICES, slot, width), BF16),
            pltpu.VMEM((experts, 2, slot, width), BF16),
            pltpu.VMEM((experts, slot, width), BF16),
            pltpu.VMEM((experts, slot, width), BF16),
            pltpu.VMEM((max(experts - 1, 1), slot, width), BF16),
            pltpu.VMEM((experts, slot, width), BF16),
            dma((3,)),
            dma((experts,)), dma((experts,)),
            dma((experts,)), dma((experts,)),
            dma((experts, 2)), dma((experts, 2)),
            dma((experts, others)), dma((experts, others)),
            dma((experts, 2)), dma((experts, 2)),
            dma((experts,)), dma((experts,)),
            dma((experts,)), dma((experts,)),
        ],
        compiler_params=pltpu.CompilerParams(
            collective_id=0, has_side_effects=True, vmem_limit_bytes=52 * 2**20
        ),
        cost_estimate=pl.CostEstimate(
            flops=6 * total * width * hid,
            bytes_accessed=6 * width * hid + 4 * block * width,
            transcendentals=total * hid,
        ),
    )(tokens, expert_ids, expert_ids.T, route_weight, w_gate, w_up, w_down)


def solution(mesh):
    placed = (
        P(("groups", "epouter"), "epinner"),
        P(("groups", "epouter"), None),
        P(("groups", "epouter"), None),
        P("epouter", "epinner", None),
        P("epouter", "epinner", None),
        P("epouter", None, "epinner"),
    )
    return jax.shard_map(
        shards,
        mesh=mesh,
        in_specs=placed,
        out_specs=P(("groups", "epouter"), "epinner"),
        check_vma=False,
    )
```

```python
import functools

import jax
import jax.numpy as jnp
from jax import lax
from jax.experimental import pallas as pl
from jax.experimental.pallas import tpu as pltpu
from jax.sharding import PartitionSpec as P

SLICES = 4
MESH = pl.DeviceIdType.MESH
F32 = jnp.float32
BF16 = jnp.bfloat16


def tile_of(width):
    return next(t for t in (512, 256, 128) if width % t == 0)


def each_tile(width, tile, body):
    @pl.loop(0, width // tile)
    def _(i):
        body(pl.ds(pl.multiple_of(i * tile, tile), tile))


def layer_kernel(
    experts, inner, slot, cuts,
    tokens, ids_t, weight_t, w_gate, w_up, w_down, out,
    w_in, w_out, outgoing, rows, own, x_send, x_recv, hidden, part, core_recv,
    y_send, y_recv, z_send, returned, mix,
    w_sem, zs, zr, ys, yr, cs, cr, xs, xr, ps, pr, qs, qr, bs, br,
):
    block, width = tokens.shape
    picks = ids_t.shape[0]
    hid = w_down.shape[1]
    here = lax.axis_index("epouter")
    expert = here // SLICES
    part_at = here % SLICES
    side = part_at % 2
    sib = part_at + 1 - 2 * side
    flip = lax.rem(part_at + 2, SLICES)
    sib_flip = lax.rem(sib + 2, SLICES)
    base = expert * SLICES
    x_at = lax.axis_index("epinner")
    piece = width // cuts
    tile = tile_of(piece)

    def at_layer(step):
        return {"epouter": lax.rem(expert + step + experts, experts) * SLICES + part_at}

    to_sib = {"epouter": base + sib}
    to_flip = {"epouter": base + flip}

    def at_inner(step):
        return {"epinner": lax.rem(x_at + step, inner)}

    loads = [
        pltpu.make_async_copy(w_gate.at[0], w_in.at[:, pl.ds(0, hid)], w_sem.at[0]),
        pltpu.make_async_copy(w_up.at[0], w_in.at[:, pl.ds(hid, hid)], w_sem.at[1]),
        pltpu.make_async_copy(w_down.at[0], w_out, w_sem.at[2]),
    ]

    barrier = pltpu.get_barrier_semaphore()
    partners = [at_layer(k) for k in range(1, experts)] + [to_sib, to_flip]
    partners += [at_inner(d) for d in range(1, inner)]
    for partner in partners:
        pl.semaphore_signal(barrier, inc=1, device_id=partner, device_id_type=MESH)

    named = lax.rem(expert + lax.broadcasted_iota(jnp.int32, (experts, block), 0), experts)
    chosen = jnp.zeros((experts, block), F32)
    coef = jnp.zeros((experts, block), F32)
    for p in range(picks):
        same = ids_t[p : p + 1, :] == named
        chosen += same.astype(F32)
        coef += jnp.where(same, weight_t[p : p + 1, :], 0.0)
    before = (
        lax.broadcasted_iota(jnp.int32, (block, block), 0)
        < lax.broadcasted_iota(jnp.int32, (block, block), 1)
    ).astype(F32)
    pos = jnp.dot(chosen.astype(BF16), before.astype(BF16), preferred_element_type=F32)
    pos = jnp.where(chosen > 0, pos, -1.0)
    slots = lax.broadcasted_iota(jnp.int32, (slot, block), 0).astype(F32)

    def gather_into(k, target):
        place = jnp.where(pos[k : k + 1, :] == slots, 1.0, 0.0).astype(BF16)
        for h in range(cuts):
            for j in range(piece // tile):
                at = h * piece + j * tile
                target[h, :, j * tile : (j + 1) * tile] = jnp.dot(
                    place, tokens[:, at : at + tile], preferred_element_type=F32
                ).astype(BF16)

    def remote(src, dst, send, recv, device):
        return pltpu.make_async_remote_copy(
            src_ref=src, dst_ref=dst, send_sem=send, recv_sem=recv,
            device_id=device, device_id_type=MESH,
        )

    def z_out(k, h):
        return remote(
            outgoing.at[k - 1, h], rows.at[k, part_at, h], zs.at[k, h], zr.at[k, h], at_layer(k)
        )

    def y_out(k, h):
        mine = rows.at[k, part_at, h]
        return remote(mine, mine, ys.at[k, h], yr.at[k, h], to_flip)

    def core_out(k, which, h):
        ref = rows.at[k, part_at if which == 0 else flip, h]
        return remote(ref, ref, cs.at[k, which, h], cr.at[k, which, h], to_sib)

    def x_out(k, d):
        return remote(
            x_send.at[k], x_recv.at[k, d - 1], xs.at[k, d - 1], xr.at[k, d - 1], at_inner(d)
        )

    def core_back(k, which, h):
        return remote(
            part.at[k, sib if which == 0 else sib_flip, h], core_recv.at[k, which, h],
            ps.at[k, which, h], pr.at[k, which, h], to_sib,
        )

    def y_back(k, h):
        return remote(y_send.at[k, h], y_recv.at[k, h], qs.at[k, h], qr.at[k, h], to_flip)

    def z_back(k, h):
        return remote(
            z_send.at[k - 1, h], returned.at[k, h], bs.at[k, h], br.at[k, h], at_layer(-k)
        )

    gather_into(0, rows.at[0, part_at])
    pl.semaphore_wait(barrier, len(partners))
    for h in range(cuts):
        y_out(0, h).start()
        core_out(0, 0, h).start()
    for k in range(1, experts):
        gather_into(k, outgoing.at[k - 1])
        if k == 1:
            for h in range(cuts):
                z_out(k, h).start()
    for load in loads:
        load.start()
    for k in range(experts):
        spread = jnp.where(pos[k : k + 1, :] == slots, coef[k : k + 1, :], 0.0)
        high = spread.astype(BF16).astype(F32)
        mix[k * slot : (k + 1) * slot, :] = jnp.concatenate([high, spread - high], axis=1)

    def arrive(k, h):
        if k >= experts:
            return
        z_out(k, h).wait_recv()
        y_out(k, h).start()
        core_out(k, 0, h).start()
        z_out(k, h).wait_send()
        if k + 1 < experts:
            z_out(k + 1, h).start()

    def forward(k, h):
        if k >= experts:
            return
        y_out(k, h).wait_recv()
        core_out(k, 1, h).start()

    def up(k):
        if k >= experts:
            return
        if k == 0:
            loads[0].wait()
            loads[1].wait()
        for h in range(cuts):
            core_out(k, 0, h).wait_recv()
            core_out(k, 1, h).wait_recv()

        def body(cols):
            value = jnp.zeros((SLICES * slot, cols.size), F32)
            for h in range(cuts):
                x = rows[k, :, h].reshape(SLICES * slot, piece)
                value += jnp.dot(
                    x, w_in[h * piece : (h + 1) * piece, cols], preferred_element_type=F32
                )
            own[k, :, cols] = value
            x_send[k, :, cols] = value.astype(BF16)

        each_tile(2 * hid, 256 if (2 * hid) % 256 == 0 else 128, body)
        for d in range(1, inner):
            x_out(k, d).start()

    def down(k):
        if not 0 <= k < experts:
            return
        for d in range(1, inner):
            x_out(k, d).wait_recv()
        if k == 0:
            loads[2].wait()

        def act(cols):
            upper = pl.ds(pl.multiple_of(cols.start + hid, 128), cols.size)
            gate = own[k, :, cols]
            lift = own[k, :, upper]
            for d in range(inner - 1):
                gate += x_recv[k, d, :, cols].astype(F32)
                lift += x_recv[k, d, :, upper].astype(F32)
            hidden[:, cols] = (gate / (1.0 + jnp.exp(-gate)) * lift).astype(BF16)

        each_tile(hid, 128, act)
        for h in range(cuts):

            def body(cols):
                above = pl.ds(pl.multiple_of(cols.start + h * piece, 128), cols.size)
                value = jnp.dot(hidden[...], w_out[:, above], preferred_element_type=F32)
                part[k, :, h, :, cols] = value.astype(BF16).reshape(SLICES, slot, tile)

            each_tile(piece, tile, body)
            core_back(k, 1, h).start()
            core_back(k, 0, h).start()

    def fold_core(k):
        if not 0 <= k < experts:
            return
        for h in range(cuts):
            core_back(k, 1, h).wait_recv()

            def body(cols):
                y_send[k, h, :, cols] = (
                    part[k, flip, h, :, cols].astype(F32)
                    + core_recv[k, 1, h, :, cols].astype(F32)
                ).astype(BF16)

            each_tile(piece, tile, body)
            y_back(k, h).start()

    def fold_y(k):
        if not 0 <= k < experts:
            return
        for h in range(cuts):
            core_back(k, 0, h).wait_recv()
            y_back(k, h).wait_recv()
            target = returned.at[0, h] if k == 0 else z_send.at[k - 1, h]

            def body(cols):
                target[:, cols] = (
                    part[k, part_at, h, :, cols].astype(F32)
                    + core_recv[k, 0, h, :, cols].astype(F32)
                    + y_recv[k, h, :, cols].astype(F32)
                ).astype(BF16)

            each_tile(piece, tile, body)
            if k:
                z_back(k, h).start()

    arrive(1, 0)
    for t in range(experts + 2):
        forward(t, 0)
        if t == 0:
            for h in range(1, cuts):
                arrive(1, h)
        down(t - 1)
        for h in range(1, cuts):
            forward(t, h)
        if t:
            arrive(t + 1, 0)
        up(t)
        fold_core(t - 1)
        if t:
            for h in range(1, cuts):
                arrive(t + 1, h)
        fold_y(t - 2)

    mixed = mix[...].T.astype(BF16)
    for h in range(cuts):
        for k in range(1, experts):
            z_back(k, h).wait_recv()

        def finish(cols):
            back = returned[:, h, :, cols].reshape(experts * slot, tile)
            both = jnp.dot(mixed, back, preferred_element_type=F32)
            above = pl.ds(pl.multiple_of(cols.start + h * piece, 128), cols.size)
            out[:, above] = (both[:block] + both[block:]).astype(BF16)

        each_tile(piece, tile, finish)

    for k in range(experts):
        for h in range(cuts):
            if k:
                z_back(k, h).wait_send()
            y_out(k, h).wait_send()
            y_back(k, h).wait_send()
            for which in range(2):
                core_out(k, which, h).wait_send()
                core_back(k, which, h).wait_send()
        for d in range(1, inner):
            x_out(k, d).wait_send()


def shards(tokens, expert_ids, route_weight, w_gate, w_up, w_down):
    experts = lax.axis_size("epouter") // SLICES
    inner = lax.axis_size("epinner")
    block, width = tokens.shape
    picks = expert_ids.shape[1]
    hid = w_down.shape[1]
    depth = min(block, 3 * block * picks // (2 * experts))
    slot = -(-depth // 16) * 16
    rows = SLICES * slot
    vmem = pl.BlockSpec(memory_space=pltpu.VMEM)
    hbm = pl.BlockSpec(memory_space=pl.ANY)
    dma = pltpu.SemaphoreType.DMA
    others = max(inner - 1, 1)
    away = max(experts - 1, 1)
    total = experts * rows
    cuts = 2
    piece = width // cuts
    return pl.pallas_call(
        functools.partial(layer_kernel, experts, inner, slot, cuts),
        out_shape=jax.ShapeDtypeStruct((block, width), BF16),
        in_specs=[vmem] * 3 + [hbm] * 3,
        out_specs=vmem,
        scratch_shapes=[
            pltpu.VMEM((width, 2 * hid), BF16),
            pltpu.VMEM((hid, width), BF16),
            pltpu.VMEM((away, cuts, slot, piece), BF16),
            pltpu.VMEM((experts, SLICES, cuts, slot, piece), BF16),
            pltpu.VMEM((experts, rows, 2 * hid), F32),
            pltpu.VMEM((experts, rows, 2 * hid), BF16),
            pltpu.VMEM((experts, others, rows, 2 * hid), BF16),
            pltpu.VMEM((rows, hid), BF16),
            pltpu.VMEM((experts, SLICES, cuts, slot, piece), BF16),
            pltpu.VMEM((experts, 2, cuts, slot, piece), BF16),
            pltpu.VMEM((experts, cuts, slot, piece), BF16),
            pltpu.VMEM((experts, cuts, slot, piece), BF16),
            pltpu.VMEM((away, cuts, slot, piece), BF16),
            pltpu.VMEM((experts, cuts, slot, piece), BF16),
            pltpu.VMEM((experts * slot, 2 * block), F32),
            dma((3,)),
            dma((experts, cuts)), dma((experts, cuts)),
            dma((experts, cuts)), dma((experts, cuts)),
            dma((experts, 2, cuts)), dma((experts, 2, cuts)),
            dma((experts, others)), dma((experts, others)),
            dma((experts, 2, cuts)), dma((experts, 2, cuts)),
            dma((experts, cuts)), dma((experts, cuts)),
            dma((experts, cuts)), dma((experts, cuts)),
        ],
        compiler_params=pltpu.CompilerParams(
            collective_id=0, has_side_effects=True, vmem_limit_bytes=52 * 2**20
        ),
        cost_estimate=pl.CostEstimate(
            flops=6 * total * width * hid,
            bytes_accessed=6 * width * hid + 4 * block * width,
            transcendentals=total * hid,
        ),
    )(tokens, expert_ids.T, route_weight.T, w_gate, w_up, w_down)


def solution(mesh):
    placed = (
        P(("groups", "epouter"), "epinner"),
        P(("groups", "epouter"), None),
        P(("groups", "epouter"), None),
        P("epouter", "epinner", None),
        P("epouter", "epinner", None),
        P("epouter", None, "epinner"),
    )
    return jax.shard_map(
        shards,
        mesh=mesh,
        in_specs=placed,
        out_specs=P(("groups", "epouter"), "epinner"),
        check_vma=False,
    )
```

```python
import functools

import jax
import jax.numpy as jnp
from jax import lax
from jax.experimental import pallas as pl
from jax.experimental.pallas import tpu as pltpu
from jax.sharding import PartitionSpec as P

SLICES = 4
MESH = pl.DeviceIdType.MESH
F32 = jnp.float32
BF16 = jnp.bfloat16


def tile_of(width):
    return next(t for t in (512, 256, 128) if width % t == 0)


def each_tile(width, tile, body):
    @pl.loop(0, width // tile)
    def _(i):
        body(pl.ds(pl.multiple_of(i * tile, tile), tile))


def layer_kernel(
    experts, inner, slot, cuts,
    tokens, ids_t, weight_t, w_gate, w_up, w_down, out,
    w_in, w_out, outgoing, rows, own, x_send, x_recv, hidden, part, core_recv,
    y_send, y_recv, z_send, returned, mix,
    w_sem, zs, zr, ys, yr, cs, cr, xs, xr, ps, pr, qs, qr, bs, br,
):
    block, width = tokens.shape
    picks = ids_t.shape[0]
    hid = w_down.shape[1]
    here = lax.axis_index("epouter")
    expert = here // SLICES
    part_at = here % SLICES
    side = part_at % 2
    sib = part_at + 1 - 2 * side
    flip = lax.rem(part_at + 2, SLICES)
    sib_flip = lax.rem(sib + 2, SLICES)
    base = expert * SLICES
    x_at = lax.axis_index("epinner")
    piece = width // cuts
    tile = tile_of(piece)

    def at_layer(step):
        return {"epouter": lax.rem(expert + step + experts, experts) * SLICES + part_at}

    to_sib = {"epouter": base + sib}
    to_flip = {"epouter": base + flip}

    def at_inner(step):
        return {"epinner": lax.rem(x_at + step, inner)}

    loads = [
        pltpu.make_async_copy(w_gate.at[0], w_in.at[:, pl.ds(0, hid)], w_sem.at[0]),
        pltpu.make_async_copy(w_up.at[0], w_in.at[:, pl.ds(hid, hid)], w_sem.at[1]),
        pltpu.make_async_copy(w_down.at[0], w_out, w_sem.at[2]),
    ]

    barrier = pltpu.get_barrier_semaphore()
    partners = [at_layer(k) for k in range(1, experts)] + [to_sib, to_flip]
    partners += [at_inner(d) for d in range(1, inner)]
    for partner in partners:
        pl.semaphore_signal(barrier, inc=1, device_id=partner, device_id_type=MESH)

    named = lax.rem(expert + lax.broadcasted_iota(jnp.int32, (experts, block), 0), experts)
    chosen = jnp.zeros((experts, block), F32)
    coef = jnp.zeros((experts, block), F32)
    for p in range(picks):
        same = ids_t[p : p + 1, :] == named
        chosen += same.astype(F32)
        coef += jnp.where(same, weight_t[p : p + 1, :], 0.0)
    before = (
        lax.broadcasted_iota(jnp.int32, (block, block), 0)
        < lax.broadcasted_iota(jnp.int32, (block, block), 1)
    ).astype(F32)
    pos = jnp.dot(chosen.astype(BF16), before.astype(BF16), preferred_element_type=F32)
    pos = jnp.where(chosen > 0, pos, -1.0)
    slots = lax.broadcasted_iota(jnp.int32, (slot, block), 0).astype(F32)

    def gather_into(k, target):
        place = jnp.where(pos[k : k + 1, :] == slots, 1.0, 0.0).astype(BF16)
        for h in range(cuts):
            for j in range(piece // tile):
                at = h * piece + j * tile
                target[h, :, j * tile : (j + 1) * tile] = jnp.dot(
                    place, tokens[:, at : at + tile], preferred_element_type=F32
                ).astype(BF16)

    def remote(src, dst, send, recv, device):
        return pltpu.make_async_remote_copy(
            src_ref=src, dst_ref=dst, send_sem=send, recv_sem=recv,
            device_id=device, device_id_type=MESH,
        )

    def z_out(k, h):
        return remote(
            outgoing.at[k - 1, h], rows.at[k, part_at, h], zs.at[k, h], zr.at[k, h], at_layer(k)
        )

    def y_out(k, h):
        mine = rows.at[k, part_at, h]
        return remote(mine, mine, ys.at[k, h], yr.at[k, h], to_flip)

    def core_out(k, which, h):
        ref = rows.at[k, part_at if which == 0 else flip, h]
        return remote(ref, ref, cs.at[k, which, h], cr.at[k, which, h], to_sib)

    def x_out(k, d):
        return remote(
            x_send.at[k], x_recv.at[k, d - 1], xs.at[k, d - 1], xr.at[k, d - 1], at_inner(d)
        )

    def core_back(k, which, h):
        return remote(
            part.at[k, sib if which == 0 else sib_flip, h], core_recv.at[k, which, h],
            ps.at[k, which, h], pr.at[k, which, h], to_sib,
        )

    def y_back(k, h):
        return remote(y_send.at[k, h], y_recv.at[k, h], qs.at[k, h], qr.at[k, h], to_flip)

    def z_back(k, h):
        return remote(
            z_send.at[k - 1, h], returned.at[k, h], bs.at[k, h], br.at[k, h], at_layer(-k)
        )

    gather_into(0, rows.at[0, part_at])
    pl.semaphore_wait(barrier, len(partners))
    for h in range(cuts):
        y_out(0, h).start()
        core_out(0, 0, h).start()
    for k in range(1, experts):
        gather_into(k, outgoing.at[k - 1])
        for h in range(cuts):
            z_out(k, h).start()
    for load in loads:
        load.start()
    for k in range(experts):
        spread = jnp.where(pos[k : k + 1, :] == slots, coef[k : k + 1, :], 0.0)
        high = spread.astype(BF16).astype(F32)
        mix[k * slot : (k + 1) * slot, :] = jnp.concatenate([high, spread - high], axis=1)

    def arrive(k, h):
        if k >= experts:
            return
        z_out(k, h).wait_recv()
        y_out(k, h).start()
        core_out(k, 0, h).start()

    def forward(k, h):
        if k >= experts:
            return
        y_out(k, h).wait_recv()
        core_out(k, 1, h).start()

    def up(k):
        if k >= experts:
            return
        if k == 0:
            loads[0].wait()
            loads[1].wait()
        for h in range(cuts):
            core_out(k, 0, h).wait_recv()
            core_out(k, 1, h).wait_recv()

        def body(cols):
            value = jnp.zeros((SLICES * slot, cols.size), F32)
            for h in range(cuts):
                x = rows[k, :, h].reshape(SLICES * slot, piece)
                value += jnp.dot(
                    x, w_in[h * piece : (h + 1) * piece, cols], preferred_element_type=F32
                )
            own[k, :, cols] = value
            x_send[k, :, cols] = value.astype(BF16)

        each_tile(2 * hid, 256 if (2 * hid) % 256 == 0 else 128, body)
        for d in range(1, inner):
            x_out(k, d).start()

    def down(k):
        if not 0 <= k < experts:
            return
        for d in range(1, inner):
            x_out(k, d).wait_recv()
        if k == 0:
            loads[2].wait()

        def act(cols):
            upper = pl.ds(pl.multiple_of(cols.start + hid, 128), cols.size)
            gate = own[k, :, cols]
            lift = own[k, :, upper]
            for d in range(inner - 1):
                gate += x_recv[k, d, :, cols].astype(F32)
                lift += x_recv[k, d, :, upper].astype(F32)
            hidden[:, cols] = (gate / (1.0 + jnp.exp(-gate)) * lift).astype(BF16)

        each_tile(hid, 128, act)
        for h in range(cuts):

            def body(cols):
                above = pl.ds(pl.multiple_of(cols.start + h * piece, 128), cols.size)
                value = jnp.dot(hidden[...], w_out[:, above], preferred_element_type=F32)
                part[k, :, h, :, cols] = value.astype(BF16).reshape(SLICES, slot, tile)

            each_tile(piece, tile, body)
            core_back(k, 1, h).start()
            core_back(k, 0, h).start()

    def fold_core(k):
        if not 0 <= k < experts:
            return
        for h in range(cuts):
            core_back(k, 1, h).wait_recv()

            def body(cols):
                y_send[k, h, :, cols] = (
                    part[k, flip, h, :, cols].astype(F32)
                    + core_recv[k, 1, h, :, cols].astype(F32)
                ).astype(BF16)

            each_tile(piece, tile, body)
            y_back(k, h).start()

    def fold_y(k):
        if not 0 <= k < experts:
            return
        for h in range(cuts):
            core_back(k, 0, h).wait_recv()
            y_back(k, h).wait_recv()
            target = returned.at[0, h] if k == 0 else z_send.at[k - 1, h]

            def body(cols):
                target[:, cols] = (
                    part[k, part_at, h, :, cols].astype(F32)
                    + core_recv[k, 0, h, :, cols].astype(F32)
                    + y_recv[k, h, :, cols].astype(F32)
                ).astype(BF16)

            each_tile(piece, tile, body)
            if k:
                z_back(k, h).start()

    for t in range(experts + 1):
        for h in range(cuts):
            arrive(t + 1, h)
            forward(t, h)
        up(t)
        if t > 2:
            fold_core(t - 2)
        if t > 3:
            fold_y(t - 3)
        down(t - 1)
    if experts > 1:
        fold_core(experts - 1)
    fold_core(0)
    for k in range(max(experts - 2, 1), experts):
        fold_y(k)
    fold_y(0)

    mixed = mix[...].T.astype(BF16)
    for h in range(cuts):
        for k in range(1, experts):
            z_back(k, h).wait_recv()

        def finish(cols):
            back = returned[:, h, :, cols].reshape(experts * slot, tile)
            both = jnp.dot(mixed, back, preferred_element_type=F32)
            above = pl.ds(pl.multiple_of(cols.start + h * piece, 128), cols.size)
            out[:, above] = (both[:block] + both[block:]).astype(BF16)

        each_tile(piece, tile, finish)

    for k in range(experts):
        for h in range(cuts):
            if k:
                z_out(k, h).wait_send()
                z_back(k, h).wait_send()
            y_out(k, h).wait_send()
            y_back(k, h).wait_send()
            for which in range(2):
                core_out(k, which, h).wait_send()
                core_back(k, which, h).wait_send()
        for d in range(1, inner):
            x_out(k, d).wait_send()


def shards(tokens, expert_ids, route_weight, w_gate, w_up, w_down):
    experts = lax.axis_size("epouter") // SLICES
    inner = lax.axis_size("epinner")
    block, width = tokens.shape
    picks = expert_ids.shape[1]
    hid = w_down.shape[1]
    depth = min(block, 3 * block * picks // (2 * experts))
    slot = -(-depth // 16) * 16
    rows = SLICES * slot
    vmem = pl.BlockSpec(memory_space=pltpu.VMEM)
    hbm = pl.BlockSpec(memory_space=pl.ANY)
    dma = pltpu.SemaphoreType.DMA
    others = max(inner - 1, 1)
    away = max(experts - 1, 1)
    total = experts * rows
    cuts = 1
    piece = width // cuts
    return pl.pallas_call(
        functools.partial(layer_kernel, experts, inner, slot, cuts),
        out_shape=jax.ShapeDtypeStruct((block, width), BF16),
        in_specs=[vmem] * 3 + [hbm] * 3,
        out_specs=vmem,
        scratch_shapes=[
            pltpu.VMEM((width, 2 * hid), BF16),
            pltpu.VMEM((hid, width), BF16),
            pltpu.VMEM((away, cuts, slot, piece), BF16),
            pltpu.VMEM((experts, SLICES, cuts, slot, piece), BF16),
            pltpu.VMEM((experts, rows, 2 * hid), F32),
            pltpu.VMEM((experts, rows, 2 * hid), BF16),
            pltpu.VMEM((experts, others, rows, 2 * hid), BF16),
            pltpu.VMEM((rows, hid), BF16),
            pltpu.VMEM((experts, SLICES, cuts, slot, piece), BF16),
            pltpu.VMEM((experts, 2, cuts, slot, piece), BF16),
            pltpu.VMEM((experts, cuts, slot, piece), BF16),
            pltpu.VMEM((experts, cuts, slot, piece), BF16),
            pltpu.VMEM((away, cuts, slot, piece), BF16),
            pltpu.VMEM((experts, cuts, slot, piece), BF16),
            pltpu.VMEM((experts * slot, 2 * block), F32),
            dma((3,)),
            dma((experts, cuts)), dma((experts, cuts)),
            dma((experts, cuts)), dma((experts, cuts)),
            dma((experts, 2, cuts)), dma((experts, 2, cuts)),
            dma((experts, others)), dma((experts, others)),
            dma((experts, 2, cuts)), dma((experts, 2, cuts)),
            dma((experts, cuts)), dma((experts, cuts)),
            dma((experts, cuts)), dma((experts, cuts)),
        ],
        compiler_params=pltpu.CompilerParams(
            collective_id=0, has_side_effects=True, vmem_limit_bytes=52 * 2**20
        ),
        cost_estimate=pl.CostEstimate(
            flops=6 * total * width * hid,
            bytes_accessed=6 * width * hid + 4 * block * width,
            transcendentals=total * hid,
        ),
    )(tokens, expert_ids.T, route_weight.T, w_gate, w_up, w_down)


def solution(mesh):
    placed = (
        P(("groups", "epouter"), "epinner"),
        P(("groups", "epouter"), None),
        P(("groups", "epouter"), None),
        P("epouter", "epinner", None),
        P("epouter", "epinner", None),
        P("epouter", None, "epinner"),
    )
    return jax.shard_map(
        shards,
        mesh=mesh,
        in_specs=placed,
        out_specs=P(("groups", "epouter"), "epinner"),
        check_vma=False,
    )
```

```python
import functools

import jax
import jax.numpy as jnp
from jax import lax
from jax.experimental import pallas as pl
from jax.experimental.pallas import tpu as pltpu
from jax.sharding import PartitionSpec as P

SLICES = 4
MESH = pl.DeviceIdType.MESH
F32 = jnp.float32
BF16 = jnp.bfloat16


def tile_of(width):
    return next(t for t in (512, 256, 128) if width % t == 0)


def each_tile(width, tile, body):
    @pl.loop(0, width // tile)
    def _(i):
        body(pl.ds(pl.multiple_of(i * tile, tile), tile))


def layer_kernel(
    experts, inner, slot, cuts,
    tokens, ids_t, weight_t, w_gate, w_up, w_down, out,
    w_in, w_out, outgoing, rows, own, x_send, x_recv, hidden, part, core_recv,
    y_send, y_recv, z_send, returned, mix,
    w_sem, zs, zr, ys, yr, cs, cr, xs, xr, ps, pr, qs, qr, bs, br,
):
    block, width = tokens.shape
    picks = ids_t.shape[0]
    hid = w_down.shape[1]
    here = lax.axis_index("epouter")
    expert = here // SLICES
    part_at = here % SLICES
    side = part_at % 2
    sib = part_at + 1 - 2 * side
    flip = lax.rem(part_at + 2, SLICES)
    sib_flip = lax.rem(sib + 2, SLICES)
    base = expert * SLICES
    x_at = lax.axis_index("epinner")
    piece = width // cuts
    tile = tile_of(piece)

    def at_layer(step):
        return {"epouter": lax.rem(expert + step + experts, experts) * SLICES + part_at}

    to_sib = {"epouter": base + sib}
    to_flip = {"epouter": base + flip}

    def at_inner(step):
        return {"epinner": lax.rem(x_at + step, inner)}

    loads = [
        pltpu.make_async_copy(w_gate.at[0], w_in.at[:, pl.ds(0, hid)], w_sem.at[0]),
        pltpu.make_async_copy(w_up.at[0], w_in.at[:, pl.ds(hid, hid)], w_sem.at[1]),
        pltpu.make_async_copy(w_down.at[0], w_out, w_sem.at[2]),
    ]

    barrier = pltpu.get_barrier_semaphore()
    partners = [at_layer(k) for k in range(1, experts)] + [to_sib, to_flip]
    partners += [at_inner(d) for d in range(1, inner)]
    for partner in partners:
        pl.semaphore_signal(barrier, inc=1, device_id=partner, device_id_type=MESH)

    named = lax.rem(expert + lax.broadcasted_iota(jnp.int32, (experts, block), 0), experts)
    chosen = jnp.zeros((experts, block), F32)
    coef = jnp.zeros((experts, block), F32)
    for p in range(picks):
        same = ids_t[p : p + 1, :] == named
        chosen += same.astype(F32)
        coef += jnp.where(same, weight_t[p : p + 1, :], 0.0)
    before = (
        lax.broadcasted_iota(jnp.int32, (block, block), 0)
        < lax.broadcasted_iota(jnp.int32, (block, block), 1)
    ).astype(F32)
    pos = jnp.dot(chosen.astype(BF16), before.astype(BF16), preferred_element_type=F32)
    pos = jnp.where(chosen > 0, pos, -1.0)
    slots = lax.broadcasted_iota(jnp.int32, (slot, block), 0).astype(F32)

    def gather_into(k, target):
        place = jnp.where(pos[k : k + 1, :] == slots, 1.0, 0.0).astype(BF16)
        for h in range(cuts):
            for j in range(piece // tile):
                at = h * piece + j * tile
                target[h, :, j * tile : (j + 1) * tile] = jnp.dot(
                    place, tokens[:, at : at + tile], preferred_element_type=F32
                ).astype(BF16)

    def remote(src, dst, send, recv, device):
        return pltpu.make_async_remote_copy(
            src_ref=src, dst_ref=dst, send_sem=send, recv_sem=recv,
            device_id=device, device_id_type=MESH,
        )

    def z_out(k, h):
        return remote(
            outgoing.at[k - 1, h], rows.at[k, part_at, h], zs.at[k, h], zr.at[k, h], at_layer(k)
        )

    def y_out(k, h):
        mine = rows.at[k, part_at, h]
        return remote(mine, mine, ys.at[k, h], yr.at[k, h], to_flip)

    def core_out(k, which, h):
        ref = rows.at[k, part_at if which == 0 else flip, h]
        return remote(ref, ref, cs.at[k, which, h], cr.at[k, which, h], to_sib)

    def x_out(k, d):
        return remote(
            x_send.at[k], x_recv.at[k, d - 1], xs.at[k, d - 1], xr.at[k, d - 1], at_inner(d)
        )

    def core_back(k, which, h):
        return remote(
            part.at[k, sib if which == 0 else sib_flip, h], core_recv.at[k, which, h],
            ps.at[k, which, h], pr.at[k, which, h], to_sib,
        )

    def y_back(k, h):
        return remote(y_send.at[k, h], y_recv.at[k, h], qs.at[k, h], qr.at[k, h], to_flip)

    def z_back(k, h):
        return remote(
            z_send.at[k - 1, h], returned.at[k, h], bs.at[k, h], br.at[k, h], at_layer(-k)
        )

    gather_into(0, rows.at[0, part_at])
    pl.semaphore_wait(barrier, len(partners))
    for h in range(cuts):
        y_out(0, h).start()
        core_out(0, 0, h).start()
    for k in range(1, experts):
        gather_into(k, outgoing.at[k - 1])
        for h in range(cuts):
            z_out(k, h).start()
    for load in loads:
        load.start()
    for k in range(experts):
        spread = jnp.where(pos[k : k + 1, :] == slots, coef[k : k + 1, :], 0.0)
        high = spread.astype(BF16).astype(F32)
        mix[k * slot : (k + 1) * slot, :] = jnp.concatenate([high, spread - high], axis=1)

    def arrive(k, h):
        if k >= experts:
            return
        z_out(k, h).wait_recv()
        y_out(k, h).start()
        core_out(k, 0, h).start()

    def forward(k, h):
        if k >= experts:
            return
        y_out(k, h).wait_recv()
        core_out(k, 1, h).start()

    def up(k):
        if k >= experts:
            return
        if k == 0:
            loads[0].wait()
            loads[1].wait()
        for h in range(cuts):
            core_out(k, 0, h).wait_recv()
            core_out(k, 1, h).wait_recv()

        def body(cols):
            value = jnp.zeros((SLICES * slot, cols.size), F32)
            for h in range(cuts):
                x = rows[k, :, h].reshape(SLICES * slot, piece)
                value += jnp.dot(
                    x, w_in[h * piece : (h + 1) * piece, cols], preferred_element_type=F32
                )
            own[k, :, cols] = value
            x_send[k, :, cols] = value.astype(BF16)

        each_tile(2 * hid, 256 if (2 * hid) % 256 == 0 else 128, body)
        for d in range(1, inner):
            x_out(k, d).start()

    def down(k):
        if not 0 <= k < experts:
            return
        for d in range(1, inner):
            x_out(k, d).wait_recv()
        if k == 0:
            loads[2].wait()

        def act(cols):
            upper = pl.ds(pl.multiple_of(cols.start + hid, 128), cols.size)
            gate = own[k, :, cols]
            lift = own[k, :, upper]
            for d in range(inner - 1):
                gate += x_recv[k, d, :, cols].astype(F32)
                lift += x_recv[k, d, :, upper].astype(F32)
            hidden[:, cols] = (gate / (1.0 + jnp.exp(-gate)) * lift).astype(BF16)

        each_tile(hid, 128, act)
        for h in range(cuts):

            def body(cols):
                above = pl.ds(pl.multiple_of(cols.start + h * piece, 128), cols.size)
                value = jnp.dot(hidden[...], w_out[:, above], preferred_element_type=F32)
                part[k, :, h, :, cols] = value.astype(BF16).reshape(SLICES, slot, tile)

            each_tile(piece, tile, body)
            core_back(k, 1, h).start()
            core_back(k, 0, h).start()

    def fold_core(k):
        if not 0 <= k < experts:
            return
        for h in range(cuts):
            core_back(k, 1, h).wait_recv()

            def body(cols):
                y_send[k, h, :, cols] = (
                    part[k, flip, h, :, cols].astype(F32)
                    + core_recv[k, 1, h, :, cols].astype(F32)
                ).astype(BF16)

            each_tile(piece, tile, body)
            y_back(k, h).start()

    def fold_y(k):
        if not 0 <= k < experts:
            return
        for h in range(cuts):
            core_back(k, 0, h).wait_recv()
            y_back(k, h).wait_recv()
            target = returned.at[0, h] if k == 0 else z_send.at[k - 1, h]

            def body(cols):
                target[:, cols] = (
                    part[k, part_at, h, :, cols].astype(F32)
                    + core_recv[k, 0, h, :, cols].astype(F32)
                    + y_recv[k, h, :, cols].astype(F32)
                ).astype(BF16)

            each_tile(piece, tile, body)
            if k:
                z_back(k, h).start()

    for t in range(experts + 1):
        for h in range(cuts):
            arrive(t + 1, h)
            forward(t, h)
        up(t)
        down(t - 1)
        if t > 1:
            fold_core(t - 1)
        if t > 2:
            fold_y(t - 2)
    if experts > 1:
        fold_y(experts - 1)
    fold_core(0)
    fold_y(0)

    mixed = mix[...].T.astype(BF16)
    for h in range(cuts):
        for k in range(1, experts):
            z_back(k, h).wait_recv()

        def finish(cols):
            back = returned[:, h, :, cols].reshape(experts * slot, tile)
            both = jnp.dot(mixed, back, preferred_element_type=F32)
            above = pl.ds(pl.multiple_of(cols.start + h * piece, 128), cols.size)
            out[:, above] = (both[:block] + both[block:]).astype(BF16)

        each_tile(piece, tile, finish)

    for k in range(experts):
        for h in range(cuts):
            if k:
                z_out(k, h).wait_send()
                z_back(k, h).wait_send()
            y_out(k, h).wait_send()
            y_back(k, h).wait_send()
            for which in range(2):
                core_out(k, which, h).wait_send()
                core_back(k, which, h).wait_send()
        for d in range(1, inner):
            x_out(k, d).wait_send()


def shards(tokens, expert_ids, route_weight, w_gate, w_up, w_down):
    experts = lax.axis_size("epouter") // SLICES
    inner = lax.axis_size("epinner")
    block, width = tokens.shape
    picks = expert_ids.shape[1]
    hid = w_down.shape[1]
    depth = min(block, 3 * block * picks // (2 * experts))
    slot = -(-depth // 16) * 16
    rows = SLICES * slot
    vmem = pl.BlockSpec(memory_space=pltpu.VMEM)
    hbm = pl.BlockSpec(memory_space=pl.ANY)
    dma = pltpu.SemaphoreType.DMA
    others = max(inner - 1, 1)
    away = max(experts - 1, 1)
    total = experts * rows
    cuts = 1
    piece = width // cuts
    return pl.pallas_call(
        functools.partial(layer_kernel, experts, inner, slot, cuts),
        out_shape=jax.ShapeDtypeStruct((block, width), BF16),
        in_specs=[vmem] * 3 + [hbm] * 3,
        out_specs=vmem,
        scratch_shapes=[
            pltpu.VMEM((width, 2 * hid), BF16),
            pltpu.VMEM((hid, width), BF16),
            pltpu.VMEM((away, cuts, slot, piece), BF16),
            pltpu.VMEM((experts, SLICES, cuts, slot, piece), BF16),
            pltpu.VMEM((experts, rows, 2 * hid), F32),
            pltpu.VMEM((experts, rows, 2 * hid), BF16),
            pltpu.VMEM((experts, others, rows, 2 * hid), BF16),
            pltpu.VMEM((rows, hid), BF16),
            pltpu.VMEM((experts, SLICES, cuts, slot, piece), BF16),
            pltpu.VMEM((experts, 2, cuts, slot, piece), BF16),
            pltpu.VMEM((experts, cuts, slot, piece), BF16),
            pltpu.VMEM((experts, cuts, slot, piece), BF16),
            pltpu.VMEM((away, cuts, slot, piece), BF16),
            pltpu.VMEM((experts, cuts, slot, piece), BF16),
            pltpu.VMEM((experts * slot, 2 * block), F32),
            dma((3,)),
            dma((experts, cuts)), dma((experts, cuts)),
            dma((experts, cuts)), dma((experts, cuts)),
            dma((experts, 2, cuts)), dma((experts, 2, cuts)),
            dma((experts, others)), dma((experts, others)),
            dma((experts, 2, cuts)), dma((experts, 2, cuts)),
            dma((experts, cuts)), dma((experts, cuts)),
            dma((experts, cuts)), dma((experts, cuts)),
        ],
        compiler_params=pltpu.CompilerParams(
            collective_id=0, has_side_effects=True, vmem_limit_bytes=52 * 2**20
        ),
        cost_estimate=pl.CostEstimate(
            flops=6 * total * width * hid,
            bytes_accessed=6 * width * hid + 4 * block * width,
            transcendentals=total * hid,
        ),
    )(tokens, expert_ids.T, route_weight.T, w_gate, w_up, w_down)


def solution(mesh):
    placed = (
        P(("groups", "epouter"), "epinner"),
        P(("groups", "epouter"), None),
        P(("groups", "epouter"), None),
        P("epouter", "epinner", None),
        P("epouter", "epinner", None),
        P("epouter", None, "epinner"),
    )
    return jax.shard_map(
        shards,
        mesh=mesh,
        in_specs=placed,
        out_specs=P(("groups", "epouter"), "epinner"),
        check_vma=False,
    )
```

```python
import functools

import jax
import jax.numpy as jnp
from jax import lax
from jax.experimental import pallas as pl
from jax.experimental.pallas import tpu as pltpu
from jax.sharding import PartitionSpec as P

SLICES = 4
MESH = pl.DeviceIdType.MESH
F32 = jnp.float32
BF16 = jnp.bfloat16


def tile_of(width):
    return next(t for t in (512, 256, 128) if width % t == 0)


def each_tile(width, tile, body):
    @pl.loop(0, width // tile)
    def _(i):
        body(pl.ds(pl.multiple_of(i * tile, tile), tile))


def layer_kernel(
    experts, inner, slot, cuts,
    tokens, ids_t, weight_t, w_gate, w_up, w_down, out,
    w_in, w_out, outgoing, rows, own, x_send, x_recv, hidden, part, core_recv,
    y_send, y_recv, z_send, returned, mix,
    w_sem, zs, zr, ys, yr, cs, cr, xs, xr, ps, pr, qs, qr, bs, br,
):
    block, width = tokens.shape
    picks = ids_t.shape[0]
    hid = w_down.shape[1]
    here = lax.axis_index("epouter")
    expert = here // SLICES
    part_at = here % SLICES
    side = part_at % 2
    sib = part_at + 1 - 2 * side
    flip = lax.rem(part_at + 2, SLICES)
    sib_flip = lax.rem(sib + 2, SLICES)
    base = expert * SLICES
    x_at = lax.axis_index("epinner")
    piece = width // cuts
    tile = tile_of(piece)

    def at_layer(step):
        return {"epouter": lax.rem(expert + step + experts, experts) * SLICES + part_at}

    to_sib = {"epouter": base + sib}
    to_flip = {"epouter": base + flip}

    def at_inner(step):
        return {"epinner": lax.rem(x_at + step, inner)}

    loads = [
        pltpu.make_async_copy(w_gate.at[0], w_in.at[:, pl.ds(0, hid)], w_sem.at[0]),
        pltpu.make_async_copy(w_up.at[0], w_in.at[:, pl.ds(hid, hid)], w_sem.at[1]),
        pltpu.make_async_copy(w_down.at[0], w_out, w_sem.at[2]),
    ]

    barrier = pltpu.get_barrier_semaphore()
    partners = [at_layer(k) for k in range(1, experts)] + [to_sib, to_flip]
    partners += [at_inner(d) for d in range(1, inner)]
    for partner in partners:
        pl.semaphore_signal(barrier, inc=1, device_id=partner, device_id_type=MESH)

    named = lax.rem(expert + lax.broadcasted_iota(jnp.int32, (experts, block), 0), experts)
    chosen = jnp.zeros((experts, block), F32)
    coef = jnp.zeros((experts, block), F32)
    for p in range(picks):
        same = ids_t[p : p + 1, :] == named
        chosen += same.astype(F32)
        coef += jnp.where(same, weight_t[p : p + 1, :], 0.0)
    before = (
        lax.broadcasted_iota(jnp.int32, (block, block), 0)
        < lax.broadcasted_iota(jnp.int32, (block, block), 1)
    ).astype(F32)
    pos = jnp.dot(chosen.astype(BF16), before.astype(BF16), preferred_element_type=F32)
    pos = jnp.where(chosen > 0, pos, -1.0)
    slots = lax.broadcasted_iota(jnp.int32, (slot, block), 0).astype(F32)

    def gather_into(k, target):
        place = jnp.where(pos[k : k + 1, :] == slots, 1.0, 0.0).astype(BF16)
        for h in range(cuts):
            for j in range(piece // tile):
                at = h * piece + j * tile
                target[h, :, j * tile : (j + 1) * tile] = jnp.dot(
                    place, tokens[:, at : at + tile], preferred_element_type=F32
                ).astype(BF16)

    def remote(src, dst, send, recv, device):
        return pltpu.make_async_remote_copy(
            src_ref=src, dst_ref=dst, send_sem=send, recv_sem=recv,
            device_id=device, device_id_type=MESH,
        )

    def z_out(k, h):
        return remote(
            outgoing.at[k - 1, h], rows.at[k, part_at, h], zs.at[k, h], zr.at[k, h], at_layer(k)
        )

    def y_out(k, h):
        mine = rows.at[k, part_at, h]
        return remote(mine, mine, ys.at[k, h], yr.at[k, h], to_flip)

    def core_out(k, which, h):
        ref = rows.at[k, part_at if which == 0 else flip, h]
        return remote(ref, ref, cs.at[k, which, h], cr.at[k, which, h], to_sib)

    def x_out(k, d):
        return remote(
            x_send.at[k], x_recv.at[k, d - 1], xs.at[k, d - 1], xr.at[k, d - 1], at_inner(d)
        )

    def core_back(k, which, h):
        return remote(
            part.at[k, sib if which == 0 else sib_flip, h], core_recv.at[k, which, h],
            ps.at[k, which, h], pr.at[k, which, h], to_sib,
        )

    def y_back(k, h):
        return remote(y_send.at[k, h], y_recv.at[k, h], qs.at[k, h], qr.at[k, h], to_flip)

    def z_back(k, h):
        return remote(
            z_send.at[k - 1, h], returned.at[k, h], bs.at[k, h], br.at[k, h], at_layer(-k)
        )

    gather_into(0, rows.at[0, part_at])
    pl.semaphore_wait(barrier, len(partners))
    for h in range(cuts):
        y_out(0, h).start()
        core_out(0, 0, h).start()
    for k in range(1, experts):
        gather_into(k, outgoing.at[k - 1])
        if k == 1:
            for h in range(cuts):
                z_out(k, h).start()
    for load in loads:
        load.start()
    for k in range(experts):
        spread = jnp.where(pos[k : k + 1, :] == slots, coef[k : k + 1, :], 0.0)
        high = spread.astype(BF16).astype(F32)
        mix[k * slot : (k + 1) * slot, :] = jnp.concatenate([high, spread - high], axis=1)

    def arrive(k, h):
        if k >= experts:
            return
        z_out(k, h).wait_recv()
        y_out(k, h).start()
        core_out(k, 0, h).start()
        if k + 1 < experts:
            z_out(k + 1, h).start()

    def forward(k, h):
        if k >= experts:
            return
        y_out(k, h).wait_recv()
        core_out(k, 1, h).start()

    def up(k):
        if k >= experts:
            return
        if k == 0:
            loads[0].wait()
            loads[1].wait()
        for h in range(cuts):
            core_out(k, 0, h).wait_recv()
            core_out(k, 1, h).wait_recv()

        def body(cols):
            value = jnp.zeros((SLICES * slot, cols.size), F32)
            for h in range(cuts):
                x = rows[k, :, h].reshape(SLICES * slot, piece)
                value += jnp.dot(
                    x, w_in[h * piece : (h + 1) * piece, cols], preferred_element_type=F32
                )
            own[k, :, cols] = value
            x_send[k, :, cols] = value.astype(BF16)

        each_tile(2 * hid, 256 if (2 * hid) % 256 == 0 else 128, body)
        for d in range(1, inner):
            x_out(k, d).start()

    def down(k):
        if not 0 <= k < experts:
            return
        for d in range(1, inner):
            x_out(k, d).wait_recv()
        if k == 0:
            loads[2].wait()

        def act(cols):
            upper = pl.ds(pl.multiple_of(cols.start + hid, 128), cols.size)
            gate = own[k, :, cols]
            lift = own[k, :, upper]
            for d in range(inner - 1):
                gate += x_recv[k, d, :, cols].astype(F32)
                lift += x_recv[k, d, :, upper].astype(F32)
            hidden[:, cols] = (gate / (1.0 + jnp.exp(-gate)) * lift).astype(BF16)

        each_tile(hid, 128, act)
        for h in range(cuts):

            def body(cols):
                above = pl.ds(pl.multiple_of(cols.start + h * piece, 128), cols.size)
                value = jnp.dot(hidden[...], w_out[:, above], preferred_element_type=F32)
                part[k, :, h, :, cols] = value.astype(BF16).reshape(SLICES, slot, tile)

            each_tile(piece, tile, body)
            core_back(k, 1, h).start()
            core_back(k, 0, h).start()

    def fold_core(k):
        if not 0 <= k < experts:
            return
        for h in range(cuts):
            core_back(k, 1, h).wait_recv()

            def body(cols):
                y_send[k, h, :, cols] = (
                    part[k, flip, h, :, cols].astype(F32)
                    + core_recv[k, 1, h, :, cols].astype(F32)
                ).astype(BF16)

            each_tile(piece, tile, body)
            y_back(k, h).start()

    def fold_y(k):
        if not 0 <= k < experts:
            return
        for h in range(cuts):
            core_back(k, 0, h).wait_recv()
            y_back(k, h).wait_recv()
            target = returned.at[0, h] if k == 0 else z_send.at[k - 1, h]

            def body(cols):
                target[:, cols] = (
                    part[k, part_at, h, :, cols].astype(F32)
                    + core_recv[k, 0, h, :, cols].astype(F32)
                    + y_recv[k, h, :, cols].astype(F32)
                ).astype(BF16)

            each_tile(piece, tile, body)
            if k:
                z_back(k, h).start()

    for t in range(experts + 1):
        for h in range(cuts):
            arrive(t + 1, h)
            forward(t, h)
        up(t)
        down(t - 1)
        if t > 1:
            fold_core(t - 1)
        if t > 2:
            fold_y(t - 2)
    if experts > 1:
        fold_y(experts - 1)
    fold_core(0)
    fold_y(0)

    mixed = mix[...].T.astype(BF16)
    for h in range(cuts):
        for k in range(1, experts):
            z_back(k, h).wait_recv()

        def finish(cols):
            back = returned[:, h, :, cols].reshape(experts * slot, tile)
            both = jnp.dot(mixed, back, preferred_element_type=F32)
            above = pl.ds(pl.multiple_of(cols.start + h * piece, 128), cols.size)
            out[:, above] = (both[:block] + both[block:]).astype(BF16)

        each_tile(piece, tile, finish)

    for k in range(experts):
        for h in range(cuts):
            if k:
                z_out(k, h).wait_send()
                z_back(k, h).wait_send()
            y_out(k, h).wait_send()
            y_back(k, h).wait_send()
            for which in range(2):
                core_out(k, which, h).wait_send()
                core_back(k, which, h).wait_send()
        for d in range(1, inner):
            x_out(k, d).wait_send()


def shards(tokens, expert_ids, route_weight, w_gate, w_up, w_down):
    experts = lax.axis_size("epouter") // SLICES
    inner = lax.axis_size("epinner")
    block, width = tokens.shape
    picks = expert_ids.shape[1]
    hid = w_down.shape[1]
    depth = min(block, 3 * block * picks // (2 * experts))
    slot = -(-depth // 16) * 16
    rows = SLICES * slot
    vmem = pl.BlockSpec(memory_space=pltpu.VMEM)
    hbm = pl.BlockSpec(memory_space=pl.ANY)
    dma = pltpu.SemaphoreType.DMA
    others = max(inner - 1, 1)
    away = max(experts - 1, 1)
    total = experts * rows
    cuts = 1
    piece = width // cuts
    return pl.pallas_call(
        functools.partial(layer_kernel, experts, inner, slot, cuts),
        out_shape=jax.ShapeDtypeStruct((block, width), BF16),
        in_specs=[vmem] * 3 + [hbm] * 3,
        out_specs=vmem,
        scratch_shapes=[
            pltpu.VMEM((width, 2 * hid), BF16),
            pltpu.VMEM((hid, width), BF16),
            pltpu.VMEM((away, cuts, slot, piece), BF16),
            pltpu.VMEM((experts, SLICES, cuts, slot, piece), BF16),
            pltpu.VMEM((experts, rows, 2 * hid), F32),
            pltpu.VMEM((experts, rows, 2 * hid), BF16),
            pltpu.VMEM((experts, others, rows, 2 * hid), BF16),
            pltpu.VMEM((rows, hid), BF16),
            pltpu.VMEM((experts, SLICES, cuts, slot, piece), BF16),
            pltpu.VMEM((experts, 2, cuts, slot, piece), BF16),
            pltpu.VMEM((experts, cuts, slot, piece), BF16),
            pltpu.VMEM((experts, cuts, slot, piece), BF16),
            pltpu.VMEM((away, cuts, slot, piece), BF16),
            pltpu.VMEM((experts, cuts, slot, piece), BF16),
            pltpu.VMEM((experts * slot, 2 * block), F32),
            dma((3,)),
            dma((experts, cuts)), dma((experts, cuts)),
            dma((experts, cuts)), dma((experts, cuts)),
            dma((experts, 2, cuts)), dma((experts, 2, cuts)),
            dma((experts, others)), dma((experts, others)),
            dma((experts, 2, cuts)), dma((experts, 2, cuts)),
            dma((experts, cuts)), dma((experts, cuts)),
            dma((experts, cuts)), dma((experts, cuts)),
        ],
        compiler_params=pltpu.CompilerParams(
            collective_id=0, has_side_effects=True, vmem_limit_bytes=52 * 2**20
        ),
        cost_estimate=pl.CostEstimate(
            flops=6 * total * width * hid,
            bytes_accessed=6 * width * hid + 4 * block * width,
            transcendentals=total * hid,
        ),
    )(tokens, expert_ids.T, route_weight.T, w_gate, w_up, w_down)


def solution(mesh):
    placed = (
        P(("groups", "epouter"), "epinner"),
        P(("groups", "epouter"), None),
        P(("groups", "epouter"), None),
        P("epouter", "epinner", None),
        P("epouter", "epinner", None),
        P("epouter", None, "epinner"),
    )
    return jax.shard_map(
        shards,
        mesh=mesh,
        in_specs=placed,
        out_specs=P(("groups", "epouter"), "epinner"),
        check_vma=False,
    )
```
